32 devices in a mesh: seq: 4 (over y, x), ctx: 8 (over z, core).
Axes of the slice: x: 2, y: 2, z: 4, core: 2. Of those that a mesh axis runs over, the one named last changes fastest.
Arguments:
- inputs: bfloat16 [4, 1024, 1024], P('seq', 'ctx'), may hold values from -6 to 6
- w_query: bfloat16 [1024, 1024], replicated, may hold values from -0.1875 to 0.1875
- w_key: bfloat16 [1024, 1024], replicated, as said below
- w_value: bfloat16 [1024, 1024], replicated, may hold values from -0.1875 to 0.1875
- damping: float32 [8, 128], replicated, may hold values from 0.25 to 4
- grad_out: bfloat16 [4, 1024, 1024], P('seq', 'ctx'), may hold values from -6 to 6
Outputs:
- grad_inputs: bfloat16 [4, 1024, 1024], P('seq', 'ctx')
- grad_weights: float32 [1024, 1024], P(('seq', 'ctx'))
The draws below stay inside these ranges and needn't reach their ends.
Inputs may be any that keep to these rules, and one draw needn't show every extreme that they name: `w_key`: entries scaled by a random factor per column.
All inputs are finite; a program needn't handle non-finite values.
Results may differ from the reference program's by a relative error of at most 0.013.
Values sent between devices are 32-bit elements; how exact they have to be, the bound alone decides.
A program may use at most 256 MiB of HBM per device.

```python
import math
import jax
import jax.numpy as jnp
from jax import lax

D = 1024
HEADS = 8
DK = 128
ITERS = 2
TOK_DEV = 128
HD = 1024
BATCH = 4
SEQLEN = 1024


def draw_w_key(key, part):
    base_key, scale_key = jax.random.split(jax.random.fold_in(key, 17))
    column_scale = jnp.exp(jax.random.uniform(scale_key, (HEADS * DK,), jnp.float32, math.log(0.1), math.log(3.0)))
    entries = jax.random.truncated_normal(base_key, -4.0, 4.0, (D, HEADS * DK), jnp.float32)
    return (entries * column_scale[None, :] / math.sqrt(D)).astype(jnp.bfloat16)


def raised(values, rng, source, target, shards_of, factor):
    def block_of(position):
        return (jnp.arange(values.shape[position]) // (values.shape[position] // shards_of)).reshape((-1,) + (1,) * (values.ndim - 1 - position))

    one_side = jax.random.permutation(rng, shards_of)[block_of(target)]
    other_side = (block_of(target) + shards_of // 2) % shards_of
    return jnp.where((block_of(source) == one_side) | (block_of(source) == other_side), factor * values, values)


def block_scale(own_key, extent, shards, low, largest):
    gain = 1.0
    for dim, blocks in shards:
        heights = jax.random.uniform(jax.random.fold_in(jax.random.fold_in(own_key, 6), dim), (blocks,), jnp.float32, low / len(shards), largest / len(shards))
        gain = gain * jnp.repeat(jnp.exp(heights), extent[dim] // blocks).reshape((-1,) + (1,) * (len(extent) - 1 - dim))
    return gain


def noise(own_key, shape, scale, most, cuts=(), dtype=jnp.bfloat16):
    level = block_scale(own_key, shape, cuts, -0.22, 0.18) if cuts else 1.0
    values = jax.random.normal(own_key, shape, jnp.float32) * scale * level
    return jnp.minimum(jnp.maximum(values, -most), most).astype(dtype)


def gaussian_with(rng, dims, scale, most, cuts, heavy, dtype=jnp.bfloat16):
    values = scale * jax.random.normal(rng, dims, jnp.float32)
    if cuts:
        values = values * block_scale(rng, dims, cuts, -0.22, 0.18)
    return jnp.clip(raised(values, jax.random.fold_in(rng, 3), *heavy), -most, most).astype(dtype)


def setup_inputs(seed: int = 0) -> dict:
    key_of = jax.random.split(jax.random.key(seed), 7)
    return {
        "inputs": gaussian_with(key_of[0], (BATCH, SEQLEN, D), 1.0, 6.0, ((0, 4), (1, 8)), (1, 2, 8, 2.0)),
        "w_query": noise(key_of[1], (D, HD), D ** -0.5, 0.1875),
        "w_key": draw_w_key(jax.random.fold_in(key_of[6], 71), 0),
        "w_value": noise(key_of[3], (D, HD), D ** -0.5, 0.1875),
        "damping": jnp.clip(jnp.exp(jax.random.uniform(key_of[4], (HEADS, DK), jnp.float32, math.log(0.25), math.log(4.0))), 0.25, 4.0),
        "grad_out": noise(key_of[5], (BATCH, SEQLEN, HD), 1.0, 6.0, ((0, 4), (1, 8))),
    }


EPSILON = 1e-06
EXACT_PRECISION = lax.Precision.HIGHEST

def unit_rows(tensor):
    inv_norm = lax.rsqrt(lax.optimization_barrier(jnp.sum(tensor * tensor, axis=-1, keepdims=True)) + EPSILON)
    return (tensor * inv_norm, inv_norm)

def unit_back(normed, inv_norm, upstream_gradient):
    return (upstream_gradient - normed * lax.optimization_barrier(jnp.sum(normed * upstream_gradient, axis=-1, keepdims=True))) * inv_norm

def causal_mask(length):
    rows_idx = lax.broadcasted_iota(jnp.int32, (length, length), 0)
    cols_idx = lax.broadcasted_iota(jnp.int32, (length, length), 1)
    return (rows_idx >= cols_idx).astype(jnp.float32)

def apply_system(vector, key_inputs, prior_state, damping, causal):
    inner = jnp.einsum('htk,hsk->hts', vector, key_inputs, precision=EXACT_PRECISION) * causal
    result = jnp.einsum('hkj,htj->htk', prior_state, vector, precision=EXACT_PRECISION)
    result = result + jnp.einsum('hts,hsk->htk', inner, key_inputs, precision=EXACT_PRECISION)
    return result + damping[:, None, :] * vector

def conjugate(target, key_inputs, prior_state, damping, causal):
    solution = jnp.zeros_like(target)
    residual = target
    direction = target
    norm_now = lax.optimization_barrier(jnp.sum(residual * residual, axis=-1, keepdims=True))
    for sweep in range(ITERS):
        image_vec = apply_system(direction, key_inputs, prior_state, damping, causal)
        step_size = norm_now / (lax.optimization_barrier(jnp.sum(direction * image_vec, axis=-1, keepdims=True)) + EPSILON)
        solution = solution + step_size * direction
        residual = residual - step_size * image_vec
        norm_next = lax.optimization_barrier(jnp.sum(residual * residual, axis=-1, keepdims=True))
        direction = residual + norm_next / (norm_now + EPSILON) * direction
        norm_now = norm_next
    return solution

def key_states(key_inputs, value_inputs):
    gram_local = jnp.einsum('htk,htj->hkj', key_inputs, key_inputs, precision=EXACT_PRECISION)
    cross_term_local = jnp.einsum('htv,htk->hvk', value_inputs, key_inputs, precision=EXACT_PRECISION)
    return (gram_local, cross_term_local)

def value_scores(upstream_gradient, value_inputs, causal):
    return jnp.einsum('htv,hsv->hts', upstream_gradient, value_inputs, precision=EXACT_PRECISION) * causal

def solve_block(normed_q, key_inputs, value_inputs, upstream_gradient, gram_prior, cross_prior, damping, causal):
    query_solution = conjugate(normed_q, key_inputs, gram_prior, damping, causal)
    scores = value_scores(upstream_gradient, value_inputs, causal)
    adjoint_rhs = jnp.einsum('hvk,htv->htk', cross_prior, upstream_gradient, precision=EXACT_PRECISION)
    adjoint_rhs = adjoint_rhs + jnp.einsum('hts,hsk->htk', scores, key_inputs, precision=EXACT_PRECISION)
    adjoint = conjugate(adjoint_rhs, key_inputs, gram_prior, damping, causal)
    return (query_solution, adjoint, scores)

def answer_states(query_solution, adjoint, upstream_gradient):
    cross_term_local = jnp.einsum('sip,sig->spg', query_solution, upstream_gradient, precision=EXACT_PRECISION)
    gram_half = jnp.einsum('htk,htj->hkj', adjoint, query_solution, precision=EXACT_PRECISION)
    return (cross_term_local, gram_half + jnp.swapaxes(gram_half, 1, 2))

def block_grads(query_solution, adjoint, scores, key_inputs, value_inputs, upstream_gradient, cross_term_after, gram_after, causal):
    query_keys = jnp.einsum('htk,hsk->hts', query_solution, key_inputs, precision=EXACT_PRECISION) * causal
    adjoint_keys = jnp.einsum('htk,hsk->hts', adjoint, key_inputs, precision=EXACT_PRECISION) * causal
    key_gradient = jnp.einsum('zrp,zwp->zwr', cross_term_after, value_inputs, precision=EXACT_PRECISION)
    key_gradient = key_gradient + jnp.einsum('hts,htk->hsk', scores, query_solution, precision=EXACT_PRECISION)
    key_gradient = key_gradient - jnp.einsum('hkj,hsj->hsk', gram_after, key_inputs, precision=EXACT_PRECISION)
    key_gradient = key_gradient - jnp.einsum('hts,htk->hsk', query_keys, adjoint, precision=EXACT_PRECISION)
    key_gradient = key_gradient - jnp.einsum('hts,htk->hsk', adjoint_keys, query_solution, precision=EXACT_PRECISION)
    value_gradient = jnp.einsum('zgf,ztg->ztf', cross_term_after, key_inputs, precision=EXACT_PRECISION)
    value_gradient = value_gradient + jnp.einsum('hts,htv->hsv', query_keys, upstream_gradient, precision=EXACT_PRECISION)
    return (key_gradient, value_gradient)

def reference(inputs, w_query, w_key, w_value, damping, grad_out):
    local_rows = inputs.reshape(BATCH * SEQLEN, D)
    query_all = jnp.dot(local_rows, w_query, preferred_element_type=jnp.float32).astype(jnp.bfloat16)
    key_all = jnp.dot(local_rows, w_key, preferred_element_type=jnp.float32).astype(jnp.bfloat16)
    value_all = jnp.dot(local_rows, w_value, preferred_element_type=jnp.float32).astype(jnp.bfloat16)
    block_count = SEQLEN // TOK_DEV
    causal = causal_mask(TOK_DEV)

    def to_blocks(tensor):
        return tensor.astype(jnp.float32).reshape(block_count, TOK_DEV, HEADS, DK).transpose(0, 2, 1, 3)

    def from_blocks(tensor):
        return tensor.transpose(0, 2, 1, 3).reshape(SEQLEN, HEADS * DK)

    def one_sequence(pieces):
        query_blocks = to_blocks(pieces[0])
        key_blocks = to_blocks(pieces[1])
        value_blocks = to_blocks(pieces[2])
        upstream_blocks = to_blocks(pieces[3])

        def forward(carried, members):
            gram_prior, cross_prior = carried
            query_rows, key_rows, value_inputs, upstream_gradient = members
            normed_q, inv_q = unit_rows(query_rows)
            key_inputs, inv_k = unit_rows(key_rows)
            gram_local, cross_term_local = key_states(key_inputs, value_inputs)
            query_solution, adjoint, scores = solve_block(normed_q, key_inputs, value_inputs, upstream_gradient, gram_prior, cross_prior, damping, causal)
            return ((gram_prior + gram_local, cross_prior + cross_term_local), (query_solution, adjoint))
        start_state = (jnp.zeros((HEADS, DK, DK), jnp.float32), jnp.zeros((HEADS, DK, DK), jnp.float32))
        unused, solved = lax.scan(forward, start_state, (query_blocks, key_blocks, value_blocks, upstream_blocks))

        def backward(carried, members):
            cross_term_after, gram_after = carried
            query_rows, key_rows, value_inputs, upstream_gradient, query_solution, adjoint = members
            normed_q, inv_q = unit_rows(query_rows)
            key_inputs, inv_k = unit_rows(key_rows)
            scores = value_scores(upstream_gradient, value_inputs, causal)
            key_gradient, value_gradient = block_grads(query_solution, adjoint, scores, key_inputs, value_inputs, upstream_gradient, cross_term_after, gram_after, causal)
            cross_term_local, gram_local = answer_states(query_solution, adjoint, upstream_gradient)
            outputs = (unit_back(normed_q, inv_q, adjoint), unit_back(key_inputs, inv_k, key_gradient), value_gradient)
            return ((cross_term_after + cross_term_local, gram_after + gram_local), outputs)
        unused_two, grads = lax.scan(backward, start_state, (query_blocks, key_blocks, value_blocks, upstream_blocks, solved[0], solved[1]), reverse=True)
        joined = jnp.concatenate([from_blocks(grads[0]), from_blocks(grads[1]), from_blocks(grads[2])], axis=1)
        return joined.astype(jnp.bfloat16)
    shaped = (query_all.reshape(BATCH, SEQLEN, HEADS * DK), key_all.reshape(BATCH, SEQLEN, HEADS * DK), value_all.reshape(BATCH, SEQLEN, HEADS * DK), grad_out)
    head_grads = lax.map(one_sequence, shaped).reshape(BATCH * SEQLEN, 3 * HEADS * DK)
    width = HEADS * DK
    summed = jnp.dot(head_grads[:, :width], w_query.T, preferred_element_type=jnp.float32)
    summed = summed + jnp.dot(head_grads[:, width:2 * width], w_key.T, preferred_element_type=jnp.float32)
    summed = summed + jnp.dot(head_grads[:, 2 * width:], w_value.T, preferred_element_type=jnp.float32)
    grad_inputs = summed.astype(jnp.bfloat16).reshape(BATCH, SEQLEN, D)
    grad_weights = jnp.dot(local_rows.T, head_grads[:, width:2 * width], preferred_element_type=jnp.float32)
    return (grad_inputs, grad_weights)
```

```python
import functools

import jax
import jax.numpy as jnp
from jax import lax
from jax.experimental import pallas as pl
from jax.experimental.pallas import tpu as pltpu
from jax.sharding import PartitionSpec as P

EPSILON = 1e-06
MESH = pl.DeviceIdType.MESH
F32 = jnp.float32
BF16 = jnp.bfloat16
NN = (((1,), (0,)), ((), ()))
NT = (((1,), (1,)), ((), ()))
TN = (((0,), (0,)), ((), ()))


def split(tensor, exact):
    high = tensor.astype(BF16)
    if not exact or tensor.dtype == BF16:
        return (high,)
    return (high, (tensor - high.astype(F32)).astype(BF16))


def mm(a, b, dims, exact=False):
    a_terms, b_terms = split(a, exact), split(b, exact)
    total = lax.dot_general(a_terms[0], b_terms[0], dims, preferred_element_type=F32)
    for term in a_terms[1:]:
        total += lax.dot_general(term, b_terms[0], dims, preferred_element_type=F32)
    for term in b_terms[1:]:
        total += lax.dot_general(a_terms[0], term, dims, preferred_element_type=F32)
    return total


def row_dot(a, b):
    return jnp.sum(a * b, axis=-1, keepdims=True)


def solve(target, keys, gram, damping, causal):
    def apply(vector):
        inner = mm(vector, keys, NT) * causal
        return mm(vector, gram, NN) + mm(inner, keys, NN) + damping * vector

    norm = row_dot(target, target)
    image = apply(target)
    step = norm / (row_dot(target, image) + EPSILON)
    answer = step * target
    residual = target - step * image
    norm_next = row_dot(residual, residual)
    direction = residual + norm_next / (norm + EPSILON) * target
    image = apply(direction)
    step = norm_next / (row_dot(direction, image) + EPSILON)
    return answer + step * direction


def unit_back(normed, inv_norm, upstream):
    return (upstream - normed * row_dot(normed, upstream)) * inv_norm


def kernel(
    ns, nz,
    x_ref, wq_ref, wk_ref, wv_ref, damp_ref, g_ref,
    gi_ref, gw_ref,
    wbuf, xf, xb, xt, gsend, gf,
    qn, rq, kn, rk, val, grad,
    loc_a, in_a, out_a, loc_b, in_b, out_b,
    dk_part, dv_part, dqkv,
    part, seq_recv, reduced, z_recv, fin, fin_recv, gi_acc, gi_recv,
    wsem, swap_send, swap_recv, a_send, a_recv, b_send, b_recv,
    s_send, s_recv, z_send, z_recv_sem, e_send, e_recv,
):
    s = lax.axis_index("seq")
    c = lax.axis_index("ctx")
    core = lax.rem(c, 2)
    chip = c // 2
    sib = c + 1 - 2 * core
    tok, width = x_ref.shape
    heads, _, size = kn.shape
    half = heads * size
    own_cols = pl.ds(pl.multiple_of(core * half, half), half)
    sib_cols = pl.ds(pl.multiple_of((1 - core) * half, half), half)
    own_rows = pl.ds(pl.multiple_of(core * tok, tok), tok)
    sib_rows = pl.ds(pl.multiple_of((1 - core) * tok, tok), tok)
    seq_block = width // ns
    z_block = seq_block // nz
    fin_rows = z_block // 2

    def remote(src, dst, send, recv, seq_id, ctx_id):
        return pltpu.make_async_remote_copy(
            src_ref=src, dst_ref=dst, send_sem=send, recv_sem=recv,
            device_id=(seq_id, ctx_id), device_id_type=MESH,
        )

    weights = [
        pltpu.make_async_copy(ref.at[:, own_cols], wbuf.at[i], wsem.at[i])
        for i, ref in enumerate((wk_ref, wv_ref, wq_ref))
    ]
    for copy in weights:
        copy.start()

    barrier = pltpu.get_barrier_semaphore()
    pl.semaphore_signal(barrier, inc=1, device_id=(s, sib), device_id_type=MESH)

    def greet_seq(i, carry):
        pl.semaphore_signal(
            barrier, inc=1, device_id=(lax.rem(s + i, ns), c), device_id_type=MESH
        )
        return carry

    def greet_z(i, carry):
        pl.semaphore_signal(
            barrier, inc=1, device_id=(s, lax.rem(chip + i, nz) * 2 + core), device_id_type=MESH
        )
        return carry

    lax.fori_loop(1, ns, greet_seq, 0)
    lax.fori_loop(1, nz, greet_z, 0)

    xf[own_rows, :] = x_ref[...].astype(F32)
    gsend[...] = g_ref[:, sib_cols].astype(F32)
    gf[own_rows, :] = g_ref[:, own_cols].astype(F32)
    pl.semaphore_wait(barrier, 1 + (ns - 1) + (nz - 1))

    swap_x = remote(xf.at[own_rows], xf.at[own_rows], swap_send.at[0], swap_recv.at[0], s, sib)
    swap_g = remote(gsend, gf.at[own_rows], swap_send.at[1], swap_recv.at[1], s, sib)
    swap_x.start()
    swap_g.start()

    @pl.when(chip == 0)
    def _():
        in_a[...] = jnp.zeros_like(in_a)

    @pl.when(chip == nz - 1)
    def _():
        in_b[...] = jnp.zeros_like(in_b)

    swap_x.wait()
    xb[...] = xf[...].astype(BF16)
    weights[0].wait()
    keys_all = jnp.dot(xb[...], wbuf[0], preferred_element_type=F32).astype(BF16).astype(F32)
    weights[1].wait()
    vals_all = jnp.dot(xb[...], wbuf[1], preferred_element_type=F32).astype(BF16)

    def unit(tensor):
        inv = lax.rsqrt(row_dot(tensor, tensor) + EPSILON)
        return tensor * inv, inv

    def link_a(h):
        return remote(out_a.at[h], in_a.at[h], a_send.at[h], a_recv.at[h], s, c + 2)

    def link_b(h):
        return remote(out_b.at[h], in_b.at[h], b_send.at[h], b_recv.at[h], s, c - 2)

    for h in range(heads):
        cols = slice(h * size, (h + 1) * size)
        normed, inv = unit(keys_all[:, cols])
        kn[h] = normed
        rk[h] = inv
        val[h] = vals_all[:, cols]
        local = mm(jnp.concatenate([normed, vals_all[:, cols].astype(F32)], axis=1), normed, TN)
        loc_a[h] = local

        @pl.when(chip == 0)
        def _():
            out_a[h] = local
            if nz > 1:
                link_a(h).start()

    weights[2].wait()
    query_all = jnp.dot(xb[...], wbuf[2], preferred_element_type=F32).astype(BF16).astype(F32)
    swap_g.wait()
    for h in range(heads):
        cols = slice(h * size, (h + 1) * size)
        normed, inv = unit(query_all[:, cols])
        qn[h] = normed
        rq[h] = inv
        grad[h] = gf[:, cols].astype(BF16)
    xt[...] = xf[...].T.astype(BF16)

    tokens = 2 * tok
    row_ids = lax.broadcasted_iota(jnp.int32, (tokens, tokens), 0)
    col_ids = lax.broadcasted_iota(jnp.int32, (tokens, tokens), 1)

    def first_pass(h, carry):
        @pl.when(chip > 0)
        def _():
            link_a(h).wait_recv()

            @pl.when(chip < nz - 1)
            def _():
                out_a[h] = in_a[h] + loc_a[h]
                link_a(h).start()

        causal = (row_ids >= col_ids).astype(F32)
        causal_t = (row_ids <= col_ids).astype(F32)
        causal_two = jnp.concatenate([causal, causal], axis=0)
        causal_two_t = jnp.concatenate([causal_t, causal_t], axis=1)
        keys, values, upstream = kn[h], val[h], grad[h]
        gram = in_a[h, :size, :]
        cross = in_a[h, size:, :]
        damping = damp_ref[pl.ds(core * heads + h, 1), :]
        scores = mm(upstream, values, NT) * causal
        rhs = mm(upstream, cross, NN) + mm(scores, keys, NN)
        answer = solve(jnp.concatenate([qn[h], rhs], axis=0), keys, gram, damping, causal_two)
        z, u = answer[:tokens], answer[tokens:]
        half_gram = mm(jnp.concatenate([u, z], axis=0), answer, TN)
        local = jnp.concatenate([half_gram, mm(z, upstream, TN)], axis=0)
        loc_b[h] = local

        @pl.when(chip == nz - 1)
        def _():
            out_b[h] = local
            if nz > 1:
                link_b(h).start()

        answer_keys = mm(keys, answer, NT) * causal_two_t
        zk_t, uk_t = answer_keys[:, :tokens], answer_keys[:, tokens:]
        scores_t = mm(values, upstream, NT) * causal_t
        dk_part[h] = mm(jnp.concatenate([scores_t - uk_t, -zk_t], axis=1), answer, NN)
        dv_part[h] = mm(zk_t, upstream, NN)
        dqkv[0, h] = unit_back(qn[h], rq[h], u).astype(BF16)
        return carry

    lax.fori_loop(0, heads, first_pass, 0)

    def seq_copy(h, i):
        peer = lax.rem(s + i, ns)
        rows = pl.ds(pl.multiple_of(peer * seq_block, seq_block), seq_block)
        return remote(
            part.at[h, rows], seq_recv.at[h, i - 1], s_send.at[h, i - 1], s_recv.at[h, i - 1],
            peer, c,
        )

    def z_copy(h, i):
        peer = lax.rem(chip + i, nz)
        rows = pl.ds(pl.multiple_of(peer * z_block, z_block), z_block)
        return remote(
            reduced.at[h, rows], z_recv.at[h, i - 1], z_send.at[h, i - 1],
            z_recv_sem.at[h, i - 1], s, peer * 2 + core,
        )

    def second_pass(h, carry):
        @pl.when(chip < nz - 1)
        def _():
            link_b(h).wait_recv()

            @pl.when(chip > 0)
            def _():
                out_b[h] = in_b[h] + loc_b[h]
                link_b(h).start()

        keys = kn[h]
        gram = in_b[h, :size, :]
        cross = in_b[h, size:, :]
        dk = dk_part[h] + mm(val[h], cross, NT) - mm(keys, gram, NN)
        dv = dv_part[h] + mm(keys, cross, NN)
        dk = unit_back(keys, rk[h], dk).astype(BF16)
        dqkv[1, h] = dk
        dqkv[2, h] = dv.astype(BF16)
        part[h] = jnp.dot(xt[...], dk, preferred_element_type=F32)
        for i in range(1, ns):
            seq_copy(h, i).start()
        return carry

    lax.fori_loop(0, heads, second_pass, 0)

    def flat(i):
        return jnp.concatenate([dqkv[i, h] for h in range(heads)], axis=1)

    total = lax.dot_general(flat(0), wbuf[2], NT, preferred_element_type=F32)
    total += lax.dot_general(flat(1), wbuf[0], NT, preferred_element_type=F32)
    total += lax.dot_general(flat(2), wbuf[1], NT, preferred_element_type=F32)
    gi_acc[...] = total
    swap_gi = remote(gi_acc.at[sib_rows], gi_recv, e_send.at[0], e_recv.at[0], s, sib)
    swap_gi.start()

    own_seq = pl.ds(pl.multiple_of(s * seq_block, seq_block), seq_block)

    def seq_reduce(h, carry):
        total = part[h, own_seq, :]
        for i in range(1, ns):
            seq_copy(h, i).wait_recv()
            total += seq_recv[h, i - 1]
        reduced[h] = total

        def send(i, carry):
            z_copy(h, i).start()
            return carry

        lax.fori_loop(1, nz, send, 0)
        return carry

    lax.fori_loop(0, heads, seq_reduce, 0)

    swap_gi.wait()
    gi_ref[...] = (gi_acc[own_rows, :] + gi_recv[...]).astype(BF16)

    own_z = pl.ds(pl.multiple_of(chip * z_block, z_block), z_block)
    for h in range(heads):

        def add(i, total):
            z_copy(h, i).wait_recv()
            return total + z_recv[h, i - 1]

        total = lax.fori_loop(1, nz, add, reduced[h, own_z, :])
        fin[:, h * size:(h + 1) * size] = total
    swap_fin = remote(fin, fin_recv, e_send.at[1], e_recv.at[1], s, sib)
    swap_fin.start()
    gw_ref[:, own_cols] = jnp.where(core == 0, fin[:fin_rows, :], fin[fin_rows:, :])

    def drain(h, carry):
        @pl.when(chip < nz - 1)
        def _():
            link_a(h).wait_send()

        @pl.when(chip > 0)
        def _():
            link_b(h).wait_send()

        for i in range(1, ns):
            seq_copy(h, i).wait_send()

        def z_wait(i, carry):
            z_copy(h, i).wait_send()
            return carry

        lax.fori_loop(1, nz, z_wait, 0)
        return carry

    lax.fori_loop(0, heads, drain, 0)
    swap_fin.wait()
    gw_ref[:, sib_cols] = jnp.where(core == 0, fin_recv[:fin_rows, :], fin_recv[fin_rows:, :])


def on_device(ns, nz, inputs, w_query, w_key, w_value, damping, grad_out):
    x, g = inputs[0], grad_out[0]
    tok, width = x.shape
    heads, size = damping.shape[0] // 2, damping.shape[1]
    tokens, half = 2 * tok, heads * size
    seq_block = width // ns
    z_block = seq_block // nz
    vmem = pltpu.VMEM
    dma = pltpu.SemaphoreType.DMA
    state = vmem((heads, 2 * size, size), F32)
    rows32 = vmem((heads, tokens, size), F32)
    rows16 = vmem((heads, tokens, size), BF16)
    norms = vmem((heads, tokens, 1), F32)
    spec = pl.BlockSpec(memory_space=pltpu.VMEM)
    hbm = pl.BlockSpec(memory_space=pl.ANY)
    grad_inputs, grad_weights = pl.pallas_call(
        functools.partial(kernel, ns, nz),
        out_shape=(
            jax.ShapeDtypeStruct((tok, width), BF16),
            jax.ShapeDtypeStruct((z_block // 2, width), F32),
        ),
        in_specs=[spec, hbm, hbm, hbm, spec, spec],
        out_specs=(spec, spec),
        scratch_shapes=[
            vmem((3, width, half), BF16),
            vmem((tokens, width), F32),
            vmem((tokens, width), BF16),
            vmem((width, tokens), BF16),
            vmem((tok, half), F32),
            vmem((tokens, half), F32),
            rows32, norms, rows32, norms, rows16, rows16,
            state, state, state, state, state, state,
            rows32, rows32,
            vmem((3, heads, tokens, size), BF16),
            vmem((heads, width, size), F32),
            vmem((heads, ns - 1, seq_block, size), F32),
            vmem((heads, seq_block, size), F32),
            vmem((heads, nz - 1, z_block, size), F32),
            vmem((z_block, half), F32),
            vmem((z_block, half), F32),
            vmem((tokens, width), F32),
            vmem((tok, width), F32),
            dma((3,)), dma((2,)), dma((2,)),
            dma((heads,)), dma((heads,)), dma((heads,)), dma((heads,)),
            dma((heads, ns - 1)), dma((heads, ns - 1)),
            dma((heads, nz - 1)), dma((heads, nz - 1)),
            dma((2,)), dma((2,)),
        ],
        compiler_params=pltpu.CompilerParams(
            collective_id=0, has_side_effects=True, vmem_limit_bytes=56 * 1024 * 1024
        ),
        name="mesa_backward",
    )(x, w_query, w_key, w_value, damping, g)
    return grad_inputs[None], grad_weights


def solution(mesh):
    in_specs = (P("seq", "ctx", None), P(), P(), P(), P(), P("seq", "ctx", None))
    out_specs = (P("seq", "ctx", None), P(("seq", "ctx"), None))
    return jax.shard_map(
        functools.partial(on_device, mesh.shape["seq"], mesh.shape["ctx"] // 2),
        mesh=mesh, in_specs=in_specs, out_specs=out_specs, check_vma=False,
    )
```

```python
import functools

import jax
import jax.numpy as jnp
from jax import lax
from jax.experimental import pallas as pl
from jax.experimental.pallas import tpu as pltpu
from jax.sharding import PartitionSpec as P

EPSILON = 1e-06
MESH = pl.DeviceIdType.MESH
F32 = jnp.float32
BF16 = jnp.bfloat16
NN = (((1,), (0,)), ((), ()))
NT = (((1,), (1,)), ((), ()))
TN = (((0,), (0,)), ((), ()))


def split(tensor, exact):
    high = tensor.astype(BF16)
    if not exact or tensor.dtype == BF16:
        return (high,)
    return (high, (tensor - high.astype(F32)).astype(BF16))


def mm(a, b, dims, exact=False):
    a_terms, b_terms = split(a, exact), split(b, exact)
    total = lax.dot_general(a_terms[0], b_terms[0], dims, preferred_element_type=F32)
    for term in a_terms[1:]:
        total += lax.dot_general(term, b_terms[0], dims, preferred_element_type=F32)
    for term in b_terms[1:]:
        total += lax.dot_general(a_terms[0], term, dims, preferred_element_type=F32)
    return total


def row_dot(a, b):
    return jnp.sum(a * b, axis=-1, keepdims=True)


def solve(target, keys, gram, damping, causal):
    def apply(vector):
        inner = mm(vector, keys, NT) * causal
        return mm(vector, gram, NN) + mm(inner, keys, NN) + damping * vector

    norm = row_dot(target, target)
    image = apply(target)
    step = norm / (row_dot(target, image) + EPSILON)
    answer = step * target
    residual = target - step * image
    norm_next = row_dot(residual, residual)
    direction = residual + norm_next / (norm + EPSILON) * target
    image = apply(direction)
    step = norm_next / (row_dot(direction, image) + EPSILON)
    return answer + step * direction


def unit_back(normed, inv_norm, upstream):
    return (upstream - normed * row_dot(normed, upstream)) * inv_norm


def kernel(
    ns, nz,
    x_ref, wq_ref, wk_ref, wv_ref, damp_ref, g_ref,
    gi_ref, gw_ref,
    wbuf, xf, xb, xt, gsend, gf,
    qn, rq, kn, rk, val, grad,
    loc_a, in_a, out_a, loc_b, in_b, out_b,
    dk_part, dv_part, dqkv,
    part, halved, passed, quartered, reduced, z_recv, fin, fin_recv, gi_acc, gi_recv,
    wsem, swap_send, swap_recv, a_send, a_recv, b_send, b_recv,
    s_send, s_recv, z_send, z_recv_sem, e_send, e_recv,
):
    s = lax.axis_index("seq")
    c = lax.axis_index("ctx")
    core = lax.rem(c, 2)
    chip = c // 2
    sib = c + 1 - 2 * core
    tok, width = x_ref.shape
    heads, _, size = kn.shape
    half = heads * size
    own_cols = pl.ds(pl.multiple_of(core * half, half), half)
    sib_cols = pl.ds(pl.multiple_of((1 - core) * half, half), half)
    own_rows = pl.ds(pl.multiple_of(core * tok, tok), tok)
    sib_rows = pl.ds(pl.multiple_of((1 - core) * tok, tok), tok)
    seq_block = width // ns
    z_block = seq_block // nz
    fin_rows = z_block // 2

    def remote(src, dst, send, recv, seq_id, ctx_id):
        return pltpu.make_async_remote_copy(
            src_ref=src, dst_ref=dst, send_sem=send, recv_sem=recv,
            device_id=(seq_id, ctx_id), device_id_type=MESH,
        )

    weights = [
        pltpu.make_async_copy(ref.at[:, own_cols], wbuf.at[i], wsem.at[i])
        for i, ref in enumerate((wk_ref, wv_ref, wq_ref))
    ]
    for copy in weights:
        copy.start()

    barrier = pltpu.get_barrier_semaphore()
    pl.semaphore_signal(barrier, inc=1, device_id=(s, sib), device_id_type=MESH)

    for peer in (lax.rem(s + 2, ns), s + 1 - 2 * lax.rem(s, 2)):
        pl.semaphore_signal(barrier, inc=1, device_id=(peer, c), device_id_type=MESH)

    def greet_z(i, carry):
        pl.semaphore_signal(
            barrier, inc=1, device_id=(s, lax.rem(chip + i, nz) * 2 + core), device_id_type=MESH
        )
        return carry

    lax.fori_loop(1, nz, greet_z, 0)

    xf[own_rows, :] = x_ref[...].astype(F32)
    gsend[...] = g_ref[:, sib_cols].astype(F32)
    gf[own_rows, :] = g_ref[:, own_cols].astype(F32)
    pl.semaphore_wait(barrier, 1 + 2 + (nz - 1))

    swap_x = remote(xf.at[own_rows], xf.at[own_rows], swap_send.at[0], swap_recv.at[0], s, sib)
    swap_g = remote(gsend, gf.at[own_rows], swap_send.at[1], swap_recv.at[1], s, sib)
    swap_x.start()
    swap_g.start()

    @pl.when(chip == 0)
    def _():
        in_a[...] = jnp.zeros_like(in_a)

    @pl.when(chip == nz - 1)
    def _():
        in_b[...] = jnp.zeros_like(in_b)

    swap_x.wait()
    xb[...] = xf[...].astype(BF16)
    weights[0].wait()
    keys_all = jnp.dot(xb[...], wbuf[0], preferred_element_type=F32).astype(BF16).astype(F32)
    weights[1].wait()
    vals_all = jnp.dot(xb[...], wbuf[1], preferred_element_type=F32).astype(BF16)

    def unit(tensor):
        inv = lax.rsqrt(row_dot(tensor, tensor) + EPSILON)
        return tensor * inv, inv

    states = (slice(0, size), slice(size, 2 * size))

    def link_a(h, k):
        rows = pl.ds(k * size, size)
        return remote(
            out_a.at[h, rows], in_a.at[h, rows], a_send.at[h, k], a_recv.at[h, k], s, c + 2
        )

    def link_b(h, k):
        rows = pl.ds(k * size, size)
        return remote(
            out_b.at[h, rows], in_b.at[h, rows], b_send.at[h, k], b_recv.at[h, k], s, c - 2
        )

    for h in range(heads):
        cols = slice(h * size, (h + 1) * size)
        normed, inv = unit(keys_all[:, cols])
        kn[h] = normed
        rk[h] = inv
        val[h] = vals_all[:, cols]
        local = mm(jnp.concatenate([normed, vals_all[:, cols].astype(F32)], axis=1), normed, TN)
        loc_a[h] = local

        @pl.when(chip == 0)
        def _():
            out_a[h] = local
            if nz > 1:
                link_a(h, 0).start()
                link_a(h, 1).start()

    weights[2].wait()
    query_all = jnp.dot(xb[...], wbuf[2], preferred_element_type=F32).astype(BF16).astype(F32)
    swap_g.wait()
    for h in range(heads):
        cols = slice(h * size, (h + 1) * size)
        normed, inv = unit(query_all[:, cols])
        qn[h] = normed
        rq[h] = inv
        grad[h] = gf[:, cols].astype(BF16)
    xt[...] = xf[...].T.astype(BF16)

    tokens = 2 * tok
    row_ids = lax.broadcasted_iota(jnp.int32, (tokens, tokens), 0)
    col_ids = lax.broadcasted_iota(jnp.int32, (tokens, tokens), 1)

    def first_pass(h, carry):
        @pl.when(chip > 0)
        def _():
            for k, rows in enumerate(states):
                link_a(h, k).wait_recv()

                @pl.when(chip < nz - 1)
                def _():
                    out_a[h, rows, :] = in_a[h, rows, :] + loc_a[h, rows, :]
                    link_a(h, k).start()

        causal = (row_ids >= col_ids).astype(F32)
        causal_t = (row_ids <= col_ids).astype(F32)
        causal_two = jnp.concatenate([causal, causal], axis=0)
        causal_two_t = jnp.concatenate([causal_t, causal_t], axis=1)
        keys, values, upstream = kn[h], val[h], grad[h]
        gram = in_a[h, :size, :]
        cross = in_a[h, size:, :]
        damping = damp_ref[pl.ds(core * heads + h, 1), :]
        scores = mm(upstream, values, NT) * causal
        rhs = mm(upstream, cross, NN) + mm(scores, keys, NN)
        answer = solve(jnp.concatenate([qn[h], rhs], axis=0), keys, gram, damping, causal_two)
        z, u = answer[:tokens], answer[tokens:]
        half_gram = mm(jnp.concatenate([u, z], axis=0), answer, TN)
        local = jnp.concatenate([half_gram, mm(z, upstream, TN)], axis=0)
        loc_b[h] = local

        @pl.when(chip == nz - 1)
        def _():
            out_b[h] = local
            if nz > 1:
                link_b(h, 0).start()
                link_b(h, 1).start()

        answer_keys = mm(keys, answer, NT) * causal_two_t
        zk_t, uk_t = answer_keys[:, :tokens], answer_keys[:, tokens:]
        scores_t = mm(values, upstream, NT) * causal_t
        dk_part[h] = mm(jnp.concatenate([scores_t - uk_t, -zk_t], axis=1), answer, NN)
        dv_part[h] = mm(zk_t, upstream, NN)
        dqkv[0, h] = unit_back(qn[h], rq[h], u).astype(BF16)
        return carry

    lax.fori_loop(0, heads, first_pass, 0)

    high, low = s // 2, lax.rem(s, 2)
    other_high, other_low = 1 - high, 1 - low

    def halve(parity, h):
        if parity == 0:
            src, peer = part.at[h, other_high], other_high * 2 + low
        else:
            src, peer = part.at[h, :, other_low], high * 2 + other_low
        return remote(src, halved.at[h], s_send.at[h, 0], s_recv.at[h, 0], peer, c)

    def quarter(parity, h):
        peer = high * 2 + other_low if parity == 0 else other_high * 2 + low
        return remote(passed.at[h], quartered.at[h], s_send.at[h, 1], s_recv.at[h, 1], peer, c)

    def z_copy(h, i):
        peer = lax.rem(chip + i, nz)
        rows = pl.ds(pl.multiple_of(peer * z_block, z_block), z_block)
        return remote(
            reduced.at[h, rows], z_recv.at[h, i - 1], z_send.at[h, i - 1],
            z_recv_sem.at[h, i - 1], s, peer * 2 + core,
        )

    def second_pass(parity, h):
        @pl.when(chip < nz - 1)
        def _():
            for k, rows in enumerate(states):
                link_b(h, k).wait_recv()

                @pl.when(chip > 0)
                def _():
                    out_b[h, rows, :] = in_b[h, rows, :] + loc_b[h, rows, :]
                    link_b(h, k).start()

        keys = kn[h]
        gram = in_b[h, :size, :]
        cross = in_b[h, size:, :]
        dk = dk_part[h] + mm(val[h], cross, NT) - mm(keys, gram, NN)
        dv = dv_part[h] + mm(keys, cross, NN)
        dk = unit_back(keys, rk[h], dk).astype(BF16)
        dqkv[1, h] = dk
        dqkv[2, h] = dv.astype(BF16)
        part[h] = jnp.dot(xt[...], dk, preferred_element_type=F32).reshape(2, 2, seq_block, size)
        halve(parity, h).start()

    def pairs(body):
        def both(pair, carry):
            body(0, 2 * pair)
            body(1, 2 * pair + 1)
            return carry

        lax.fori_loop(0, heads // 2, both, 0)


    def pass_on(parity, h):
        halve(parity, h).wait_recv()
        if parity == 0:
            passed[h] = part[h, high, other_low] + halved[h, other_low]
        else:
            passed[h] = part[h, other_high, low] + halved[h, other_high]
        quarter(parity, h).start()

    def reduce(parity, h):
        kept = part[h, high, low] + halved[h, low if parity == 0 else high]
        quarter(parity, h).wait_recv()
        reduced[h] = kept + quartered[h]

        def send(i, carry):
            z_copy(h, i).start()
            return carry

        lax.fori_loop(1, nz, send, 0)

    second_pass(0, 0)
    second_pass(1, 1)
    for h in range(2, heads):
        second_pass(h % 2, h)
        pass_on(h % 2, h - 2)

    def flat(i):
        return jnp.concatenate([dqkv[i, h] for h in range(heads)], axis=1)

    total = lax.dot_general(flat(0), wbuf[2], NT, preferred_element_type=F32)
    total += lax.dot_general(flat(1), wbuf[0], NT, preferred_element_type=F32)
    total += lax.dot_general(flat(2), wbuf[1], NT, preferred_element_type=F32)
    gi_acc[...] = total
    swap_gi = remote(gi_acc.at[sib_rows], gi_recv, e_send.at[0], e_recv.at[0], s, sib)
    swap_gi.start()

    for h in range(2, heads):
        pass_on(h % 2, h)
        reduce(h % 2, h - 2)
    for h in range(heads - 2, heads):
        reduce(h % 2, h)

    swap_gi.wait()
    gi_ref[...] = (gi_acc[own_rows, :] + gi_recv[...]).astype(BF16)

    own_z = pl.ds(pl.multiple_of(chip * z_block, z_block), z_block)
    for h in range(heads):

        def add(i, total):
            z_copy(h, i).wait_recv()
            return total + z_recv[h, i - 1]

        total = lax.fori_loop(1, nz, add, reduced[h, own_z, :])
        fin[:, h * size:(h + 1) * size] = total
    swap_fin = remote(fin, fin_recv, e_send.at[1], e_recv.at[1], s, sib)
    swap_fin.start()
    gw_ref[:, own_cols] = jnp.where(core == 0, fin[:fin_rows, :], fin[fin_rows:, :])

    def drain(parity, h):
        @pl.when(chip < nz - 1)
        def _():
            link_a(h, 0).wait_send()
            link_a(h, 1).wait_send()

        @pl.when(chip > 0)
        def _():
            link_b(h, 0).wait_send()
            link_b(h, 1).wait_send()

        halve(parity, h).wait_send()
        quarter(parity, h).wait_send()

        def z_wait(i, carry):
            z_copy(h, i).wait_send()
            return carry

        lax.fori_loop(1, nz, z_wait, 0)

    pairs(drain)
    swap_fin.wait()
    gw_ref[:, sib_cols] = jnp.where(core == 0, fin_recv[:fin_rows, :], fin_recv[fin_rows:, :])


def hand_on(gi_in, gw_in, gi_ref, gw_ref):
    gi_ref[...] = gi_in[...]
    gw_ref[...] = gw_in[...]


def on_device(ns, nz, inputs, w_query, w_key, w_value, damping, grad_out):
    x, g = inputs[0], grad_out[0]
    if ns != 4 or damping.shape[0] % 4:
        raise ValueError("seq size")
    tok, width = x.shape
    heads, size = damping.shape[0] // 2, damping.shape[1]
    tokens, half = 2 * tok, heads * size
    seq_block = width // ns
    z_block = seq_block // nz
    vmem = pltpu.VMEM
    dma = pltpu.SemaphoreType.DMA
    state = vmem((heads, 2 * size, size), F32)
    rows32 = vmem((heads, tokens, size), F32)
    rows16 = vmem((heads, tokens, size), BF16)
    norms = vmem((heads, tokens, 1), F32)
    spec = pl.BlockSpec(memory_space=pltpu.VMEM)
    hbm = pl.BlockSpec(memory_space=pl.ANY)
    grad_inputs, grad_weights = pl.pallas_call(
        functools.partial(kernel, ns, nz),
        out_shape=(
            jax.ShapeDtypeStruct((tok, width), BF16),
            jax.ShapeDtypeStruct((z_block // 2, width), F32),
        ),
        in_specs=[spec, hbm, hbm, hbm, spec, spec],
        out_specs=(spec, spec),
        scratch_shapes=[
            vmem((3, width, half), BF16),
            vmem((tokens, width), F32),
            vmem((tokens, width), BF16),
            vmem((width, tokens), BF16),
            vmem((tok, half), F32),
            vmem((tokens, half), F32),
            rows32, norms, rows32, norms, rows16, rows16,
            state, state, state, state, state, state,
            rows32, rows32,
            vmem((3, heads, tokens, size), BF16),
            vmem((heads, 2, 2, seq_block, size), F32),
            vmem((heads, 2, seq_block, size), F32),
            vmem((heads, seq_block, size), F32),
            vmem((heads, seq_block, size), F32),
            vmem((heads, seq_block, size), F32),
            vmem((heads, nz - 1, z_block, size), F32),
            vmem((z_block, half), F32),
            vmem((z_block, half), F32),
            vmem((tokens, width), F32),
            vmem((tok, width), F32),
            dma((3,)), dma((2,)), dma((2,)),
            dma((heads, 2)), dma((heads, 2)), dma((heads, 2)), dma((heads, 2)),
            dma((heads, 2)), dma((heads, 2)),
            dma((heads, nz - 1)), dma((heads, nz - 1)),
            dma((2,)), dma((2,)),
        ],
        compiler_params=pltpu.CompilerParams(
            collective_id=0, has_side_effects=True, vmem_limit_bytes=56 * 1024 * 1024
        ),
        name="mesa_backward",
    )(x, w_query, w_key, w_value, damping, g)
    grad_inputs, grad_weights = pl.pallas_call(
        hand_on,
        out_shape=(
            jax.ShapeDtypeStruct(grad_inputs.shape, BF16),
            jax.ShapeDtypeStruct(grad_weights.shape, F32),
        ),
        in_specs=[spec, spec],
        out_specs=(spec, spec),
        name="hand_on",
    )(grad_inputs, grad_weights)
    return grad_inputs[None], grad_weights


def solution(mesh):
    in_specs = (P("seq", "ctx", None), P(), P(), P(), P(), P("seq", "ctx", None))
    out_specs = (P("seq", "ctx", None), P(("seq", "ctx"), None))
    return jax.shard_map(
        functools.partial(on_device, mesh.shape["seq"], mesh.shape["ctx"] // 2),
        mesh=mesh, in_specs=in_specs, out_specs=out_specs, check_vma=False,
    )
```
